128 devices in a mesh: row: 32 (over y, z, x_lo), col: 4 (over x_hi, core).
Axes of the slice: x: 4 (x_hi: 2, x_lo: 2; x = x_hi * 2 + x_lo), y: 4, z: 4, core: 2. Of those that a mesh axis runs over, the one named last changes fastest.
Arguments:
- pair: bfloat16 [1536, 1536, 128], P('row', 'col'), may hold values from -6 to 6
- w_in: bfloat16 [128, 512], replicated, may hold values from -0.5 to 0.5
- w_gate: bfloat16 [128, 128], replicated, may hold values from -0.5 to 0.5
- w_out: bfloat16 [128, 128], replicated, may hold values from -0.5 to 0.5
Outputs:
- swapped: bfloat16 [1536, 1536, 128], P('row', 'col')
The draws below stay inside these ranges and needn't reach their ends.
All inputs are finite; a program needn't handle non-finite values.
Results may differ from the reference program's by a relative error of at most 0.0053.
Values may be sent and summed in bfloat16 or wider, within the bound.
No kernel may reach another device: no remote copies, remote signals or barrier semaphores. Data moves between devices by JAX's collectives and lax.ppermute only.
A program may use at most 192 MiB of HBM per device.

```python
import jax
import jax.numpy as jnp
from jax import lax

C = 128
H = 128
R_DEV = 48
TOKENS = 1536


def block_levels(own_key, dims, split, low, high):
    def one(position, blocks):
        steps = jax.random.uniform(jax.random.fold_in(jax.random.fold_in(own_key, 6), position), (blocks,), jnp.float32, low / len(split), high / len(split))
        return jnp.repeat(jnp.exp(steps), dims[position] // blocks).reshape((-1,) + (1,) * (len(dims) - position - 1))

    gain = one(*split[0])
    for cut in split[1:]:
        gain = gain * one(*cut)
    return gain


def normal_values(key, shape, scale, limit, pieces=(), held_as=jnp.bfloat16):
    entries = jax.random.normal(key, shape, jnp.float32) * scale
    if len(pieces) > 0:
        entries = block_levels(key, shape, pieces, -0.22, 0.18) * entries
    return jnp.clip(entries, min=-limit, max=limit).astype(held_as)


def setup_inputs(seed: int = 0) -> dict:
    key_of = jax.random.split(jax.random.key(seed), 5)
    return {
        "pair": normal_values(key_of[0], (TOKENS, TOKENS, C), 1.0, 6.0, ((0, 32), (1, 4))),
        "w_in": normal_values(key_of[1], (C, 4 * H), C ** -0.5, 0.5),
        "w_gate": normal_values(key_of[2], (C, C), C ** -0.5, 0.5),
        "w_out": normal_values(key_of[3], (H, C), H ** -0.5, 0.5),
    }


def normalize(values):
    mean = lax.optimization_barrier(jnp.mean(values, axis=-1, keepdims=True))
    centred = values - mean
    spread = lax.optimization_barrier(jnp.mean(centred * centred, axis=-1, keepdims=True))
    return centred * lax.rsqrt(spread + 1e-05)

def combine(z_rows, x_rows, w_gate, w_out):
    width = z_rows.shape[-1]
    hidden = x_rows.shape[-1]
    z_float = z_rows.astype(jnp.float32)
    normed = normalize(z_float).astype(jnp.bfloat16)
    gate = jax.nn.sigmoid(jnp.dot(normed.reshape(-1, width), w_gate, preferred_element_type=jnp.float32))
    x_normed = normalize(x_rows.astype(jnp.float32)).astype(jnp.bfloat16)
    update = jnp.dot(x_normed.reshape(-1, hidden), w_out, preferred_element_type=jnp.float32)
    merged = z_float.reshape(-1, width) + gate * update
    return merged.reshape(z_rows.shape).astype(jnp.bfloat16)

def reference(pair, w_in, w_gate, w_out):
    blocks = TOKENS // R_DEV

    def project(index):
        rows = lax.dynamic_slice_in_dim(pair, index * R_DEV, R_DEV, 0)
        normed = normalize(rows.astype(jnp.float32)).astype(jnp.bfloat16)
        proj = jnp.dot(normed.reshape(-1, C), w_in, preferred_element_type=jnp.float32)
        proj = proj.reshape(R_DEV, TOKENS, 4 * H)
        left = (jax.nn.sigmoid(proj[..., :H]) * proj[..., H:2 * H]).astype(jnp.bfloat16)
        right = (jax.nn.sigmoid(proj[..., 2 * H:3 * H]) * proj[..., 3 * H:]).astype(jnp.bfloat16)
        return (jnp.transpose(left, (2, 0, 1)), jnp.transpose(right, (2, 0, 1)))
    left_all, right_all = lax.map(project, jnp.arange(blocks, dtype=jnp.int32))
    left_all = jnp.transpose(left_all, (1, 0, 2, 3)).reshape(H, TOKENS, TOKENS)
    right_all = jnp.transpose(right_all, (1, 0, 2, 3)).reshape(H, TOKENS, TOKENS)

    def channel(planes):
        return jnp.dot(planes[0], planes[1].T, preferred_element_type=jnp.float32).astype(jnp.bfloat16)
    crossed = lax.map(channel, (left_all, right_all))

    def finish(index):
        start = index * R_DEV
        columns = lax.dynamic_slice_in_dim(pair, start, R_DEV, 1)
        z_rows = jnp.transpose(columns, (1, 0, 2))
        piece = lax.dynamic_slice_in_dim(crossed, start, R_DEV, 2)
        x_rows = jnp.transpose(piece, (2, 1, 0))
        return combine(z_rows, x_rows, w_gate, w_out)
    result = lax.map(finish, jnp.arange(blocks, dtype=jnp.int32))
    return result.reshape(TOKENS, TOKENS, C)
```

```python
import jax
import jax.numpy as jnp
from jax import lax
from jax.experimental import pallas as pl
from jax.experimental.pallas import tpu as pltpu
from jax.sharding import PartitionSpec as P

ALL = ("row", "col")
VMEM_LIMIT = 56 * 1024 * 1024


def sigmoid(x):
    return 0.5 * jnp.tanh(0.5 * x) + 0.5


def params():
    return pltpu.CompilerParams(vmem_limit_bytes=VMEM_LIMIT)


def project_kernel(x_ref, wt_ref, a_ref, b_ref, sa, sb):
    groups = x_ref.shape[0]
    hidden = a_ref.shape[0]

    for g in range(0, groups, 2):
        parts = []
        for q in range(2):
            v = x_ref[g + q].T.astype(jnp.float32)
            mean = jnp.mean(v, axis=0, keepdims=True)
            v = v - mean
            var = jnp.mean(v * v, axis=0, keepdims=True)
            parts.append((v * lax.rsqrt(var + 1e-5)).astype(jnp.bfloat16))
        n = jnp.concatenate(parts, axis=1)
        for dst, k in ((sa, 0), (sb, 2)):
            gate = jnp.dot(wt_ref[pl.ds(k * hidden, hidden), :], n, preferred_element_type=jnp.float32)
            value = jnp.dot(
                wt_ref[pl.ds((k + 1) * hidden, hidden), :], n, preferred_element_type=jnp.float32
            )
            res = sigmoid(gate) * value
            for q in range(2):
                dst[pl.ds(g + q, hidden, stride=groups), :] = res[:, q * 128 : (q + 1) * 128]
    a_ref[...] = sa[...].astype(jnp.bfloat16).reshape(a_ref.shape)
    b_ref[...] = sb[...].astype(jnp.bfloat16).reshape(b_ref.shape)


def project(pair, w_in):
    rows, cols, width = pair.shape
    hidden = w_in.shape[1] // 4
    kg = cols // 128
    gb = 16
    out = jax.ShapeDtypeStruct((hidden, kg, rows, 128), jnp.bfloat16)
    spec = pl.BlockSpec((hidden, None, gb, 128), lambda k, i: (0, k, i, 0))
    return pl.pallas_call(
        project_kernel,
        grid=(kg, rows // gb),
        in_specs=[
            pl.BlockSpec((gb, 128, width), lambda k, i: (i, k, 0)),
            pl.BlockSpec((4 * hidden, width), lambda k, i: (0, 0)),
        ],
        out_specs=[spec, spec],
        out_shape=[out, out],
        scratch_shapes=[pltpu.VMEM((hidden * gb, 128), jnp.float32)] * 2,
        compiler_params=params(),
        cost_estimate=pl.CostEstimate(
            flops=2 * rows * cols * width * hidden * 4,
            bytes_accessed=6 * rows * cols * width,
            transcendentals=2 * rows * cols * hidden,
        ),
        name="project",
    )(pair, w_in.T)


def cross_kernel(b_ref, a_ref, o_ref):
    nb, kgs, rows, _ = b_ref.shape
    na = a_ref.shape[0]
    b = jnp.concatenate(
        [b_ref[:, q].reshape(nb * rows, 128) for q in range(kgs)], axis=1
    )
    step = o_ref.shape[2] * 128 // rows
    for c in range(na // step):
        a = jnp.concatenate(
            [a_ref[pl.ds(c * step, step), q].reshape(step * rows, 128) for q in range(kgs)], axis=1
        )
        res = lax.dot_general(b, a, (((1,), (1,)), ((), ())), preferred_element_type=jnp.float32)
        res = res.astype(jnp.bfloat16)
        for t in range(o_ref.shape[2]):
            o_ref[:, c, t] = res[:, t * 128 : (t + 1) * 128].reshape(nb, rows, 128)


def cross(b_recv, a_recv, row_count, col_count):
    _, kg, rows, _ = b_recv.shape
    b = b_recv.reshape(row_count, col_count * kg, rows, 128)
    a = a_recv.reshape(row_count, col_count * kg, rows, 128)
    kgs = col_count * kg
    nb = 8
    tokens = row_count * rows
    return pl.pallas_call(
        cross_kernel,
        grid=(row_count // nb,),
        in_specs=[
            pl.BlockSpec((nb, kgs, rows, 128), lambda j: (j, 0, 0, 0)),
            pl.BlockSpec((row_count, kgs, rows, 128), lambda j: (0, 0, 0, 0)),
        ],
        out_specs=pl.BlockSpec((nb, col_count, kg, rows, 128), lambda j: (j, 0, 0, 0, 0)),
        out_shape=jax.ShapeDtypeStruct((row_count, col_count, kg, rows, 128), jnp.bfloat16),
        compiler_params=params(),
        cost_estimate=pl.CostEstimate(
            flops=2 * tokens**3, bytes_accessed=6 * tokens * tokens, transcendentals=0
        ),
        name="cross",
    )(b, a)


def gate_kernel(z_ref, w_ref, g_ref):
    jb, cols, width = z_ref.shape
    z = z_ref[...].reshape(jb * cols, width).astype(jnp.float32)
    mean = jnp.mean(z, axis=-1, keepdims=True)
    z = z - mean
    var = jnp.mean(z * z, axis=-1, keepdims=True)
    n = (z * lax.rsqrt(var + 1e-5)).astype(jnp.bfloat16)
    g_ref[...] = sigmoid(
        jnp.dot(n, w_ref[...], preferred_element_type=jnp.float32)
    ).reshape(g_ref.shape)


def gate_of(z, w_gate):
    rows, cols, width = z.shape
    jb = 4
    return pl.pallas_call(
        gate_kernel,
        grid=(rows // jb,),
        in_specs=[
            pl.BlockSpec((jb, cols, width), lambda j: (j, 0, 0)),
            pl.BlockSpec((width, width), lambda j: (0, 0)),
        ],
        out_specs=pl.BlockSpec((jb, cols, width), lambda j: (j, 0, 0)),
        out_shape=jax.ShapeDtypeStruct((rows, cols, width), jnp.float32),
        compiler_params=params(),
        cost_estimate=pl.CostEstimate(
            flops=2 * rows * cols * width * width,
            bytes_accessed=6 * rows * cols * width,
            transcendentals=rows * cols * width,
        ),
        name="gate",
    )(z, w_gate)


def finish_kernel(r_ref, z_ref, g_ref, w_ref, o_ref, s0, s1, s2):
    hidden, groups, jb, _ = r_ref.shape
    scr = (s0, s1, s2)
    for t in range(groups):
        scr[t][...] = r_ref[:, t].astype(jnp.float32).reshape(hidden * jb, 128)
    for j in range(jb):
        for t in range(groups):
            v = scr[t][pl.ds(j, hidden, stride=jb), :]
            mean = jnp.mean(v, axis=0, keepdims=True)
            v = v - mean
            var = jnp.mean(v * v, axis=0, keepdims=True)
            n = (v * lax.rsqrt(var + 1e-5)).astype(jnp.bfloat16)
            update = lax.dot_general(
                n, w_ref[...], (((0,), (0,)), ((), ())), preferred_element_type=jnp.float32
            )
            at = pl.ds(t * 128, 128)
            res = z_ref[j, at].astype(jnp.float32) + g_ref[j, at] * update
            o_ref[j, at] = res.astype(jnp.bfloat16)


def finish(returned, z, gate, w_out):
    hidden, groups, rows, _ = returned.shape
    _, cols, width = z.shape
    jb = 16
    tok = pl.BlockSpec((jb, cols, width), lambda j: (j, 0, 0))
    return pl.pallas_call(
        finish_kernel,
        grid=(rows // jb,),
        in_specs=[
            pl.BlockSpec((hidden, groups, jb, 128), lambda j: (0, 0, j, 0)),
            tok,
            tok,
            pl.BlockSpec((hidden, width), lambda j: (0, 0)),
        ],
        out_specs=tok,
        out_shape=jax.ShapeDtypeStruct((rows, cols, width), jnp.bfloat16),
        scratch_shapes=[pltpu.VMEM((hidden * jb, 128), jnp.float32)] * 3,
        compiler_params=params(),
        cost_estimate=pl.CostEstimate(
            flops=2 * rows * cols * width * hidden,
            bytes_accessed=10 * rows * cols * width,
            transcendentals=0,
        ),
        name="finish",
    )(returned, z, gate, w_out)


def swap_tokens(pair, row_count, col_count):
    rows, cols, width = pair.shape
    low = row_count // col_count
    me = lax.rem(lax.axis_index("row"), low)
    pieces = pair.reshape(rows, low, rows, width)
    got = jnp.zeros((low, rows, rows, width), pair.dtype)
    for s in range(low):
        perm = [
            ((h * low + q) * col_count + c, (c * low + (q ^ s)) * col_count + h)
            for h in range(col_count)
            for q in range(low)
            for c in range(col_count)
        ]
        other = lax.bitwise_xor(me, s)
        piece = lax.dynamic_index_in_dim(pieces, other, 1, keepdims=False)
        moved = lax.ppermute(piece, ALL, perm)
        got = lax.dynamic_update_index_in_dim(got, moved, other, 0)
    return jnp.transpose(got, (2, 0, 1, 3)).reshape(rows, cols, width)


def exchange(x):
    return lax.all_to_all(x, ALL, split_axis=0, concat_axis=0, tiled=True)


def on_device(pair, w_in, w_gate, w_out):
    row_count = lax.axis_size("row")
    col_count = lax.axis_size("col")
    turned = swap_tokens(pair, row_count, col_count)
    a, b = project(pair, w_in)
    a_own = exchange(a)
    b_own = exchange(b)
    crossed = cross(b_own, a_own, row_count, col_count)
    crossed = crossed.reshape((row_count * col_count,) + crossed.shape[2:])
    returned = exchange(crossed)
    return finish(returned, turned, gate_of(turned, w_gate), w_out)


def solution(mesh):
    placed = (P("row", "col", None), P(), P(), P())
    return jax.shard_map(
        on_device, mesh=mesh, in_specs=placed, out_specs=P("row", "col", None), check_vma=False
    )
```

```python
import jax
import jax.numpy as jnp
from jax import lax
from jax.experimental import pallas as pl
from jax.experimental.pallas import tpu as pltpu
from jax.sharding import PartitionSpec as P

ALL = ("row", "col")
GB = 16
EARLY = 7
VMEM_LIMIT = 56 * 1024 * 1024


def sigmoid(x):
    return 0.5 * jnp.tanh(0.5 * x) + 0.5


def params():
    return pltpu.CompilerParams(vmem_limit_bytes=VMEM_LIMIT)


def project_kernel(x_ref, wt_ref, o_ref, sa, sb):
    groups = x_ref.shape[0]
    hidden = o_ref.shape[0]

    for g in range(0, groups, 2):
        parts = []
        for q in range(2):
            v = x_ref[g + q].T.astype(jnp.float32)
            mean = jnp.mean(v, axis=0, keepdims=True)
            v = v - mean
            var = jnp.mean(v * v, axis=0, keepdims=True)
            parts.append((v * lax.rsqrt(var + 1e-5)).astype(jnp.bfloat16))
        n = jnp.concatenate(parts, axis=1)
        for dst, k in ((sa, 0), (sb, 2)):
            gate = jnp.dot(wt_ref[pl.ds(k * hidden, hidden), :], n, preferred_element_type=jnp.float32)
            value = jnp.dot(
                wt_ref[pl.ds((k + 1) * hidden, hidden), :], n, preferred_element_type=jnp.float32
            )
            res = sigmoid(gate) * value
            for q in range(2):
                dst[pl.ds(g + q, hidden, stride=groups), :] = res[:, q * 128 : (q + 1) * 128]
    for p, src in ((0, sa), (1, sb)):
        o_ref[:, p] = src[...].astype(jnp.bfloat16).reshape(hidden, groups, 128)


def project(pair, w_in):
    rows, cols, width = pair.shape
    hidden = w_in.shape[1] // 4
    kg = cols // 128
    return pl.pallas_call(
        project_kernel,
        grid=(kg, rows // GB),
        in_specs=[
            pl.BlockSpec((GB, 128, width), lambda k, i: (i, k, 0)),
            pl.BlockSpec((4 * hidden, width), lambda k, i: (0, 0)),
        ],
        out_specs=pl.BlockSpec((hidden, None, None, 2, GB, 128), lambda k, i: (0, k, i, 0, 0, 0)),
        out_shape=jax.ShapeDtypeStruct((hidden, kg, rows // GB, 2, GB, 128), jnp.bfloat16),
        scratch_shapes=[pltpu.VMEM((hidden * GB, 128), jnp.float32)] * 2,
        compiler_params=params(),
        cost_estimate=pl.CostEstimate(
            flops=2 * rows * cols * width * hidden * 4,
            bytes_accessed=6 * rows * cols * width,
            transcendentals=2 * rows * cols * hidden,
        ),
        name="project",
    )(pair, w_in.T)


def plane_rows(ref, first, count):
    _, kgs, parts, group, lanes = ref.shape
    return jnp.concatenate(
        [ref[pl.ds(first, count), q].reshape(count * parts * group, lanes) for q in range(kgs)],
        axis=1,
    )


def cross_kernel(b_ref, a_ref, o_ref):
    nb, col_count, kg, rows, _ = o_ref.shape
    b = plane_rows(b_ref, 0, nb)
    step = kg * 128 // rows
    for c in range(col_count):
        a = plane_rows(a_ref, c * step, step)
        res = lax.dot_general(b, a, (((1,), (1,)), ((), ())), preferred_element_type=jnp.float32)
        res = res.astype(jnp.bfloat16)
        for t in range(kg):
            o_ref[:, c, t] = res[:, t * 128 : (t + 1) * 128].reshape(nb, rows, 128)


def cross(own, row_count, col_count):
    _, kg, parts, _, group, _ = own.shape
    rows = parts * group
    kgs = col_count * kg
    own = own.reshape(row_count, kgs, parts, 2, group, 128)
    nb = 8
    tokens = row_count * rows
    return pl.pallas_call(
        cross_kernel,
        grid=(row_count // nb,),
        in_specs=[
            pl.BlockSpec((nb, kgs, parts, None, group, 128), lambda j: (j, 0, 0, 1, 0, 0)),
            pl.BlockSpec((row_count, kgs, parts, None, group, 128), lambda j: (0, 0, 0, 0, 0, 0)),
        ],
        out_specs=pl.BlockSpec((nb, col_count, kg, rows, 128), lambda j: (j, 0, 0, 0, 0)),
        out_shape=jax.ShapeDtypeStruct((row_count, col_count, kg, rows, 128), jnp.bfloat16),
        compiler_params=params(),
        cost_estimate=pl.CostEstimate(
            flops=2 * tokens**3, bytes_accessed=6 * tokens * tokens, transcendentals=0
        ),
        name="cross",
    )(own, own).reshape(row_count * col_count, kg, rows, 128)


def gate_kernel(z_ref, w_ref, g_ref):
    jb, cols, width = z_ref.shape
    z = z_ref[...].reshape(jb * cols, width).astype(jnp.float32)
    mean = jnp.mean(z, axis=-1, keepdims=True)
    z = z - mean
    var = jnp.mean(z * z, axis=-1, keepdims=True)
    n = (z * lax.rsqrt(var + 1e-5)).astype(jnp.bfloat16)
    g_ref[...] = sigmoid(
        jnp.dot(n, w_ref[...], preferred_element_type=jnp.float32)
    ).reshape(g_ref.shape)


def gate_of(z, w_gate):
    rows, cols, width = z.shape
    jb = 4
    return pl.pallas_call(
        gate_kernel,
        grid=(rows // jb,),
        in_specs=[
            pl.BlockSpec((jb, cols, width), lambda j: (j, 0, 0)),
            pl.BlockSpec((width, width), lambda j: (0, 0)),
        ],
        out_specs=pl.BlockSpec((jb, cols, width), lambda j: (j, 0, 0)),
        out_shape=jax.ShapeDtypeStruct((rows, cols, width), jnp.float32),
        compiler_params=params(),
        cost_estimate=pl.CostEstimate(
            flops=2 * rows * cols * width * width,
            bytes_accessed=6 * rows * cols * width,
            transcendentals=rows * cols * width,
        ),
        name="gate",
    )(z, w_gate)


def finish_kernel(r_ref, z_ref, g_ref, w_ref, o_ref, scr):
    hidden, jb, _ = r_ref.shape
    scr[...] = r_ref[...].astype(jnp.float32).reshape(hidden * jb, 128)
    for j in range(jb):
        v = scr[pl.ds(j, hidden, stride=jb), :]
        mean = jnp.mean(v, axis=0, keepdims=True)
        v = v - mean
        var = jnp.mean(v * v, axis=0, keepdims=True)
        n = (v * lax.rsqrt(var + 1e-5)).astype(jnp.bfloat16)
        update = lax.dot_general(
            n, w_ref[...], (((0,), (0,)), ((), ())), preferred_element_type=jnp.float32
        )
        o_ref[j] = (z_ref[j].astype(jnp.float32) + g_ref[j] * update).astype(jnp.bfloat16)


def finish(returned, z, gate, w_out):
    hidden, groups, rows, _ = returned.shape
    _, cols, width = z.shape
    tok = pl.BlockSpec((GB, 128, width), lambda j, t: (j, t, 0))
    return pl.pallas_call(
        finish_kernel,
        grid=(rows // GB, groups),
        in_specs=[
            pl.BlockSpec((hidden, None, GB, 128), lambda j, t: (0, t, j, 0)),
            tok,
            tok,
            pl.BlockSpec((hidden, width), lambda j, t: (0, 0)),
        ],
        out_specs=tok,
        out_shape=jax.ShapeDtypeStruct((rows, cols, width), jnp.bfloat16),
        scratch_shapes=[pltpu.VMEM((hidden * GB, 128), jnp.float32)],
        compiler_params=params(),
        cost_estimate=pl.CostEstimate(
            flops=2 * rows * cols * width * hidden,
            bytes_accessed=10 * rows * cols * width,
            transcendentals=0,
        ),
        name="finish",
    )(returned, z, gate, w_out)


def cut(pair, low):
    rows, cols, width = pair.shape
    me = lax.rem(lax.axis_index("row"), low)
    pieces = pair.reshape(rows, low, rows, width)
    return [
        lax.dynamic_index_in_dim(pieces, lax.bitwise_xor(me, s), 1, keepdims=False)
        for s in range(low)
    ]


def send(piece, s, low, high):
    perm = [
        ((h * low + q) * high + c, (c * low + (q ^ s)) * high + h)
        for h in range(high)
        for q in range(low)
        for c in range(high)
    ]
    return lax.ppermute(piece, ALL, perm)


def place(moved):
    low = len(moved)
    rows, _, width = moved[0].shape
    me = lax.rem(lax.axis_index("row"), low)
    got = jnp.zeros((low, rows, rows, width), moved[0].dtype)
    for s, piece in enumerate(moved):
        got = lax.dynamic_update_index_in_dim(got, piece, lax.bitwise_xor(me, s), 0)
    return jnp.transpose(got, (2, 0, 1, 3)).reshape(rows, low * rows, width)


def exchange(x):
    return lax.all_to_all(x, ALL, split_axis=0, concat_axis=0, tiled=True)


def on_device(pair, w_in, w_gate, w_out):
    row_count = lax.axis_size("row")
    col_count = lax.axis_size("col")
    low = row_count // col_count
    pieces = cut(pair, low)
    early = [send(pieces[s], s, low, col_count) for s in range(EARLY)]
    early, both = lax.optimization_barrier((early, project(pair, w_in)))
    own = exchange(both)
    own, rest = lax.optimization_barrier((own, pieces[EARLY:]))
    late = [send(p, EARLY + s, low, col_count) for s, p in enumerate(rest)]
    late, crossed = lax.optimization_barrier((late, cross(own, row_count, col_count)))
    returned = exchange(crossed)
    turned = place(early + late)
    return finish(returned, turned, gate_of(turned, w_gate), w_out)


def solution(mesh):
    placed = (P("row", "col", None), P(), P(), P())
    return jax.shard_map(
        on_device, mesh=mesh, in_specs=placed, out_specs=P("row", "col", None), check_vma=False
    )
```

```python
import jax
import jax.numpy as jnp
from jax import lax
from jax.experimental import pallas as pl
from jax.experimental.pallas import tpu as pltpu
from jax.sharding import PartitionSpec as P

ALL = ("row", "col")
GB = 16


def sigmoid(x):
    return 0.5 * jnp.tanh(0.5 * x) + 0.5


def params(mib):
    return pltpu.CompilerParams(vmem_limit_bytes=mib * 1024 * 1024)


def project_kernel(x_ref, wt_ref, o_ref, sa, sb):
    groups = x_ref.shape[0]
    hidden = o_ref.shape[0]

    for g in range(0, groups, 2):
        parts = []
        for q in range(2):
            v = x_ref[g + q].T.astype(jnp.float32)
            mean = jnp.mean(v, axis=0, keepdims=True)
            v = v - mean
            var = jnp.mean(v * v, axis=0, keepdims=True)
            parts.append((v * lax.rsqrt(var + 1e-5)).astype(jnp.bfloat16))
        n = jnp.concatenate(parts, axis=1)
        for dst, k in ((sa, 0), (sb, 2)):
            gate = jnp.dot(wt_ref[pl.ds(k * hidden, hidden), :], n, preferred_element_type=jnp.float32)
            value = jnp.dot(
                wt_ref[pl.ds((k + 1) * hidden, hidden), :], n, preferred_element_type=jnp.float32
            )
            res = sigmoid(gate) * value
            for q in range(2):
                dst[pl.ds(g + q, hidden, stride=groups), :] = res[:, q * 128 : (q + 1) * 128]
    for p, src in ((0, sa), (1, sb)):
        o_ref[:, p] = src[...].astype(jnp.bfloat16).reshape(hidden, groups, 128)


def project(pair, w_in):
    rows, cols, width = pair.shape
    hidden = w_in.shape[1] // 4
    kg = cols // 128
    return pl.pallas_call(
        project_kernel,
        grid=(kg, rows // GB),
        in_specs=[
            pl.BlockSpec((GB, 128, width), lambda k, i: (i, k, 0)),
            pl.BlockSpec((4 * hidden, width), lambda k, i: (0, 0)),
        ],
        out_specs=pl.BlockSpec((hidden, None, None, 2, GB, 128), lambda k, i: (0, k, i, 0, 0, 0)),
        out_shape=jax.ShapeDtypeStruct((hidden, kg, rows // GB, 2, GB, 128), jnp.bfloat16),
        scratch_shapes=[pltpu.VMEM((hidden * GB, 128), jnp.float32)] * 2,
        compiler_params=params(16),
        cost_estimate=pl.CostEstimate(
            flops=2 * rows * cols * width * hidden * 4,
            bytes_accessed=6 * rows * cols * width,
            transcendentals=2 * rows * cols * hidden,
        ),
        name="project",
    )(pair, w_in.T)


def plane_rows(ref, first, count):
    _, kgs, parts, group, lanes = ref.shape
    return jnp.concatenate(
        [ref[pl.ds(first, count), q].reshape(count * parts * group, lanes) for q in range(kgs)],
        axis=1,
    )


def cross_kernel(b_ref, a_ref, o_ref):
    nb, col_count, kg, rows, _ = o_ref.shape
    b = plane_rows(b_ref, 0, nb)
    step = kg * 128 // rows
    for c in range(col_count):
        a = plane_rows(a_ref, c * step, step)
        res = lax.dot_general(b, a, (((1,), (1,)), ((), ())), preferred_element_type=jnp.float32)
        res = res.astype(jnp.bfloat16)
        for t in range(kg):
            o_ref[:, c, t] = res[:, t * 128 : (t + 1) * 128].reshape(nb, rows, 128)


def cross(own, row_count, col_count):
    _, kg, parts, _, group, _ = own.shape
    rows = parts * group
    kgs = col_count * kg
    own = own.reshape(row_count, kgs, parts, 2, group, 128)
    nb = 8
    tokens = row_count * rows
    return pl.pallas_call(
        cross_kernel,
        grid=(row_count // nb,),
        in_specs=[
            pl.BlockSpec((nb, kgs, parts, None, group, 128), lambda j: (j, 0, 0, 1, 0, 0)),
            pl.BlockSpec((row_count, kgs, parts, None, group, 128), lambda j: (0, 0, 0, 0, 0, 0)),
        ],
        out_specs=pl.BlockSpec((nb, col_count, kg, rows, 128), lambda j: (j, 0, 0, 0, 0)),
        out_shape=jax.ShapeDtypeStruct((row_count, col_count, kg, rows, 128), jnp.bfloat16),
        compiler_params=params(56),
        cost_estimate=pl.CostEstimate(
            flops=2 * tokens**3, bytes_accessed=6 * tokens * tokens, transcendentals=0
        ),
        name="cross",
    )(own, own).reshape(row_count * col_count, kg, rows, 128)


def gate_kernel(z_ref, w_ref, g_ref):
    jb, cols, width = z_ref.shape
    z = z_ref[...].reshape(jb * cols, width).astype(jnp.float32)
    mean = jnp.mean(z, axis=-1, keepdims=True)
    z = z - mean
    var = jnp.mean(z * z, axis=-1, keepdims=True)
    n = (z * lax.rsqrt(var + 1e-5)).astype(jnp.bfloat16)
    gate = sigmoid(jnp.dot(n, w_ref[...], preferred_element_type=jnp.float32))
    g_ref[...] = gate.astype(g_ref.dtype).reshape(g_ref.shape)


def gate_of(z, w_gate):
    rows, cols, width = z.shape
    jb = 4
    return pl.pallas_call(
        gate_kernel,
        grid=(rows // jb,),
        in_specs=[
            pl.BlockSpec((jb, cols, width), lambda j: (j, 0, 0)),
            pl.BlockSpec((width, width), lambda j: (0, 0)),
        ],
        out_specs=pl.BlockSpec((jb, cols, width), lambda j: (j, 0, 0)),
        out_shape=jax.ShapeDtypeStruct((rows, cols, width), jnp.bfloat16),
        compiler_params=params(12),
        cost_estimate=pl.CostEstimate(
            flops=2 * rows * cols * width * width,
            bytes_accessed=6 * rows * cols * width,
            transcendentals=rows * cols * width,
        ),
        name="gate",
    )(z, w_gate)


def finish_kernel(r_ref, z_ref, g_ref, w_ref, o_ref, scr):
    hidden, jb, _ = r_ref.shape
    width = w_ref.shape[1]
    batch = 4
    scr[...] = r_ref[...].astype(jnp.float32).reshape(hidden * jb, 128)
    for first in range(0, jb, batch):
        parts = []
        for j in range(first, first + batch):
            v = scr[pl.ds(j, hidden, stride=jb), :]
            mean = jnp.mean(v, axis=0, keepdims=True)
            v = v - mean
            var = jnp.mean(v * v, axis=0, keepdims=True)
            parts.append((v * lax.rsqrt(var + 1e-5)).astype(jnp.bfloat16))
        update = lax.dot_general(
            jnp.concatenate(parts, axis=1),
            w_ref[...],
            (((0,), (0,)), ((), ())),
            preferred_element_type=jnp.float32,
        ).reshape(batch, 128, width)
        at = pl.ds(first, batch)
        o_ref[at] = (z_ref[at].astype(jnp.float32) + g_ref[at].astype(jnp.float32) * update).astype(jnp.bfloat16)


def finish(returned, z, gate, w_out):
    hidden, groups, rows, _ = returned.shape
    _, cols, width = z.shape
    tok = pl.BlockSpec((GB, 128, width), lambda j, t: (j, t, 0))
    return pl.pallas_call(
        finish_kernel,
        grid=(rows // GB, groups),
        in_specs=[
            pl.BlockSpec((hidden, None, GB, 128), lambda j, t: (0, t, j, 0)),
            tok,
            tok,
            pl.BlockSpec((hidden, width), lambda j, t: (0, 0)),
        ],
        out_specs=tok,
        out_shape=jax.ShapeDtypeStruct((rows, cols, width), jnp.bfloat16),
        scratch_shapes=[pltpu.VMEM((hidden * GB, 128), jnp.float32)],
        compiler_params=params(56),
        cost_estimate=pl.CostEstimate(
            flops=2 * rows * cols * width * hidden,
            bytes_accessed=10 * rows * cols * width,
            transcendentals=0,
        ),
        name="finish",
    )(returned, z, gate, w_out)


def cut(pair, low):
    rows, cols, width = pair.shape
    me = lax.rem(lax.axis_index("row"), low)
    pieces = pair.reshape(rows, low, rows, width)
    return [
        lax.dynamic_index_in_dim(pieces, lax.bitwise_xor(me, s), 1, keepdims=False)
        for s in range(low)
    ]


def send(piece, low, high, target, chosen=lambda h, q, c: True):
    perm = []
    for h in range(high):
        for q in range(low):
            for c in range(high):
                if chosen(h, q, c):
                    th, tq, tc = target(h, q, c)
                    perm.append(((h * low + q) * high + c, (th * low + tq) * high + tc))
    return lax.ppermute(piece, ALL, perm)


def near(h, q, c):
    return h // 2 == c // 2


def far(h, q, c):
    return not near(h, q, c)


def final(s):
    return lambda h, q, c: (c, q ^ s, h)


def halfway(s):
    return lambda h, q, c: (c, q ^ s, c // 2 * 2 + h % 2)


def onward(h, q, c):
    return h, q, c ^ 2


def place(moved):
    low = len(moved)
    rows, _, width = moved[0].shape
    me = lax.rem(lax.axis_index("row"), low)
    got = jnp.zeros((low, rows, rows, width), moved[0].dtype)
    for s, piece in enumerate(moved):
        got = lax.dynamic_update_index_in_dim(got, piece, lax.bitwise_xor(me, s), 0)
    return jnp.transpose(got, (2, 0, 1, 3)).reshape(rows, low * rows, width)


def exchange(x):
    return lax.all_to_all(x, ALL, split_axis=0, concat_axis=0, tiled=True)


def on_device(pair, w_in, w_gate, w_out):
    row_count = lax.axis_size("row")
    high = lax.axis_size("col")
    low = row_count // high
    rows = pair.shape[0]
    is_far = lax.axis_index("row") // low // 2 != lax.axis_index("col") // 2
    p = cut(pair, low)

    def direct(s, piece):
        return send(piece, low, high, final(s))

    def inner(s, piece):
        return send(piece, low, high, final(s), near)

    def first_leg(s, piece):
        return send(piece, low, high, halfway(s), far)

    def second_leg(piece):
        return send(piece, low, high, onward, near)

    half0, half1 = first_leg(0, p[0]), first_leg(1, p[1])
    got = {s: direct(s, p[s]) for s in (2, 3, 4)}
    half0, half1, p0, p1, p5, p6, p7 = lax.optimization_barrier((half0, half1, p[0], p[1], p[5], p[6], p[7]))
    leg = second_leg(jnp.concatenate([half0, half1], axis=0))
    got[5], got[6] = direct(5, p5), direct(6, p6)
    in0, in1 = inner(0, p0), inner(1, p1)
    got, leg, in0, in1, p7, both = lax.optimization_barrier(
        (got, leg, in0, in1, p7, project(pair, w_in))
    )
    own = exchange(both)
    own, p7 = lax.optimization_barrier((own, p7))
    got[7], crossed = lax.optimization_barrier((direct(7, p7), cross(own, row_count, high)))
    returned = exchange(crossed)
    got[0] = jnp.where(is_far, leg[:rows], in0)
    got[1] = jnp.where(is_far, leg[rows:], in1)
    turned = place([got[s] for s in range(low)])
    return finish(returned, turned, gate_of(turned, w_gate), w_out)


def solution(mesh):
    placed = (P("row", "col", None), P(), P(), P())
    return jax.shard_map(
        on_device, mesh=mesh, in_specs=placed, out_specs=P("row", "col", None), check_vma=False
    )
```

```python
import jax
import jax.numpy as jnp
from jax import lax
from jax.experimental import pallas as pl
from jax.experimental.pallas import tpu as pltpu
from jax.sharding import PartitionSpec as P

ALL = ("row", "col")
GB = 16


def sigmoid(x):
    return 0.5 * jnp.tanh(0.5 * x) + 0.5


def params(mib):
    return pltpu.CompilerParams(vmem_limit_bytes=mib * 1024 * 1024)


def project_kernel(x_ref, wt_ref, o_ref, sa, sb):
    groups = x_ref.shape[0]
    hidden = o_ref.shape[0]

    for g in range(0, groups, 2):
        parts = []
        for q in range(2):
            v = x_ref[g + q].T.astype(jnp.float32)
            mean = jnp.mean(v, axis=0, keepdims=True)
            v = v - mean
            var = jnp.mean(v * v, axis=0, keepdims=True)
            parts.append((v * lax.rsqrt(var + 1e-5)).astype(jnp.bfloat16))
        n = jnp.concatenate(parts, axis=1)
        for dst, k in ((sa, 0), (sb, 2)):
            gate = jnp.dot(wt_ref[pl.ds(k * hidden, hidden), :], n, preferred_element_type=jnp.float32)
            value = jnp.dot(
                wt_ref[pl.ds((k + 1) * hidden, hidden), :], n, preferred_element_type=jnp.float32
            )
            res = sigmoid(gate) * value
            for q in range(2):
                dst[pl.ds(g + q, hidden, stride=groups), :] = res[:, q * 128 : (q + 1) * 128]
    for p, src in ((0, sa), (1, sb)):
        o_ref[:, p] = src[...].astype(jnp.bfloat16).reshape(hidden, groups, 128)


def project(pair, w_in):
    rows, cols, width = pair.shape
    hidden = w_in.shape[1] // 4
    kg = cols // 128
    return pl.pallas_call(
        project_kernel,
        grid=(kg, rows // GB),
        in_specs=[
            pl.BlockSpec((GB, 128, width), lambda k, i: (i, k, 0)),
            pl.BlockSpec((4 * hidden, width), lambda k, i: (0, 0)),
        ],
        out_specs=pl.BlockSpec((hidden, None, None, 2, GB, 128), lambda k, i: (0, k, i, 0, 0, 0)),
        out_shape=jax.ShapeDtypeStruct((hidden, kg, rows // GB, 2, GB, 128), jnp.bfloat16),
        scratch_shapes=[pltpu.VMEM((hidden * GB, 128), jnp.float32)] * 2,
        compiler_params=params(16),
        cost_estimate=pl.CostEstimate(
            flops=2 * rows * cols * width * hidden * 4,
            bytes_accessed=6 * rows * cols * width,
            transcendentals=2 * rows * cols * hidden,
        ),
        name="project",
    )(pair, w_in.T)


def plane_rows(ref, first, count):
    _, kgs, parts, group, lanes = ref.shape
    return jnp.concatenate(
        [ref[pl.ds(first, count), q].reshape(count * parts * group, lanes) for q in range(kgs)],
        axis=1,
    )


def cross_kernel(b_ref, a_ref, o_ref):
    nb, col_count, parts, kg, group, _ = o_ref.shape
    rows = parts * group
    b = plane_rows(b_ref, 0, nb)
    step = kg * 128 // rows
    for c in range(col_count):
        a = plane_rows(a_ref, c * step, step)
        res = lax.dot_general(b, a, (((1,), (1,)), ((), ())), preferred_element_type=jnp.float32)
        res = res.astype(jnp.bfloat16)
        for t in range(kg):
            o_ref[:, c, :, t] = res[:, t * 128 : (t + 1) * 128].reshape(nb, parts, group, 128)


def cross(own, row_count, col_count):
    _, kg, parts, _, group, _ = own.shape
    rows = parts * group
    kgs = col_count * kg
    own = own.reshape(row_count, kgs, parts, 2, group, 128)
    nb = 8
    tokens = row_count * rows
    return pl.pallas_call(
        cross_kernel,
        grid=(row_count // nb,),
        in_specs=[
            pl.BlockSpec((nb, kgs, parts, None, group, 128), lambda j: (j, 0, 0, 1, 0, 0)),
            pl.BlockSpec((row_count, kgs, parts, None, group, 128), lambda j: (0, 0, 0, 0, 0, 0)),
        ],
        out_specs=pl.BlockSpec(
            (nb, col_count, parts, kg, group, 128), lambda j: (j, 0, 0, 0, 0, 0)
        ),
        out_shape=jax.ShapeDtypeStruct(
            (row_count, col_count, parts, kg, group, 128), jnp.bfloat16
        ),
        compiler_params=params(56),
        cost_estimate=pl.CostEstimate(
            flops=2 * tokens**3, bytes_accessed=6 * tokens * tokens, transcendentals=0
        ),
        name="cross",
    )(own, own).reshape(row_count * col_count, parts, kg, group, 128)


def gate_kernel(z_ref, w_ref, g_ref):
    jb, cols, width = z_ref.shape
    z = z_ref[...].reshape(jb * cols, width).astype(jnp.float32)
    mean = jnp.mean(z, axis=-1, keepdims=True)
    z = z - mean
    var = jnp.mean(z * z, axis=-1, keepdims=True)
    n = (z * lax.rsqrt(var + 1e-5)).astype(jnp.bfloat16)
    gate = sigmoid(jnp.dot(n, w_ref[...], preferred_element_type=jnp.float32))
    g_ref[...] = gate.astype(g_ref.dtype).reshape(g_ref.shape)


def gate_of(z, w_gate):
    rows, cols, width = z.shape
    jb = 4
    return pl.pallas_call(
        gate_kernel,
        grid=(rows // jb,),
        in_specs=[
            pl.BlockSpec((jb, cols, width), lambda j: (j, 0, 0)),
            pl.BlockSpec((width, width), lambda j: (0, 0)),
        ],
        out_specs=pl.BlockSpec((jb, cols, width), lambda j: (j, 0, 0)),
        out_shape=jax.ShapeDtypeStruct((rows, cols, width), jnp.bfloat16),
        compiler_params=params(12),
        cost_estimate=pl.CostEstimate(
            flops=2 * rows * cols * width * width,
            bytes_accessed=6 * rows * cols * width,
            transcendentals=rows * cols * width,
        ),
        name="gate",
    )(z, w_gate)


def finish_kernel(r_ref, z_ref, g_ref, w_ref, o_ref, scr):
    hidden, groups, jb, _ = r_ref.shape
    width = w_ref.shape[1]
    batch = 4
    for t in range(groups):
        scr[...] = r_ref[:, t].astype(jnp.float32).reshape(hidden * jb, 128)
        for first in range(0, jb, batch):
            parts = []
            for j in range(first, first + batch):
                v = scr[pl.ds(j, hidden, stride=jb), :]
                mean = jnp.mean(v, axis=0, keepdims=True)
                v = v - mean
                var = jnp.mean(v * v, axis=0, keepdims=True)
                parts.append((v * lax.rsqrt(var + 1e-5)).astype(jnp.bfloat16))
            update = lax.dot_general(
                jnp.concatenate(parts, axis=1),
                w_ref[...],
                (((0,), (0,)), ((), ())),
                preferred_element_type=jnp.float32,
            ).reshape(batch, 128, width)
            at = (pl.ds(first, batch), pl.ds(t * 128, 128))
            res = z_ref[at].astype(jnp.float32) + g_ref[at].astype(jnp.float32) * update
            o_ref[at] = res.astype(jnp.bfloat16)


def finish(returned, z, gate, w_out):
    hidden, parts, groups, jb, _ = returned.shape
    rows, cols, width = z.shape
    tok = pl.BlockSpec((jb, cols, width), lambda j: (j, 0, 0))
    return pl.pallas_call(
        finish_kernel,
        grid=(parts,),
        in_specs=[
            pl.BlockSpec((hidden, None, groups, jb, 128), lambda j: (0, j, 0, 0, 0)),
            tok,
            tok,
            pl.BlockSpec((hidden, width), lambda j: (0, 0)),
        ],
        out_specs=tok,
        out_shape=jax.ShapeDtypeStruct((rows, cols, width), jnp.bfloat16),
        scratch_shapes=[pltpu.VMEM((hidden * jb, 128), jnp.float32)],
        compiler_params=params(56),
        cost_estimate=pl.CostEstimate(
            flops=2 * rows * cols * width * hidden,
            bytes_accessed=8 * rows * cols * width,
            transcendentals=0,
        ),
        name="finish",
    )(returned, z, gate, w_out)


def cut(pair, low):
    rows, cols, width = pair.shape
    me = lax.rem(lax.axis_index("row"), low)
    pieces = pair.reshape(rows, low, rows, width)
    return [
        lax.dynamic_index_in_dim(pieces, lax.bitwise_xor(me, s), 1, keepdims=False)
        for s in range(low)
    ]


def send(piece, low, high, target, chosen=lambda h, q, c: True):
    perm = []
    for h in range(high):
        for q in range(low):
            for c in range(high):
                if chosen(h, q, c):
                    th, tq, tc = target(h, q, c)
                    perm.append(((h * low + q) * high + c, (th * low + tq) * high + tc))
    return lax.ppermute(piece, ALL, perm)


def near(h, q, c):
    return h // 2 == c // 2


def far(h, q, c):
    return not near(h, q, c)


def final(s):
    return lambda h, q, c: (c, q ^ s, h)


def halfway(s):
    return lambda h, q, c: (c, q ^ s, c // 2 * 2 + h % 2)


def onward(h, q, c):
    return h, q, c ^ 2


def place(moved):
    low = len(moved)
    rows, _, width = moved[0].shape
    me = lax.rem(lax.axis_index("row"), low)
    got = jnp.zeros((low, rows, rows, width), moved[0].dtype)
    for s, piece in enumerate(moved):
        got = lax.dynamic_update_index_in_dim(got, piece, lax.bitwise_xor(me, s), 0)
    return jnp.transpose(got, (2, 0, 1, 3)).reshape(rows, low * rows, width)


def exchange(x):
    return lax.all_to_all(x, ALL, split_axis=0, concat_axis=0, tiled=True)


def on_device(pair, w_in, w_gate, w_out):
    row_count = lax.axis_size("row")
    high = lax.axis_size("col")
    low = row_count // high
    rows = pair.shape[0]
    is_far = lax.axis_index("row") // low // 2 != lax.axis_index("col") // 2
    p = cut(pair, low)

    def direct(s, piece):
        return send(piece, low, high, final(s))

    def inner(s, piece):
        return send(piece, low, high, final(s), near)

    def first_leg(s, piece):
        return send(piece, low, high, halfway(s), far)

    def second_leg(piece):
        return send(piece, low, high, onward, near)

    half0, half1 = first_leg(0, p[0]), first_leg(1, p[1])
    got = {s: direct(s, p[s]) for s in (2, 3)}
    in0 = inner(0, p[0])
    half0, half1, rest = lax.optimization_barrier((half0, half1, [p[s] for s in (1, 4, 5, 6, 7)]))
    leg = second_leg(jnp.concatenate([half0, half1], axis=0))
    for s in (4, 5, 6):
        got[s] = direct(s, rest[s - 3])
    in1 = inner(1, rest[0])
    got, leg, in0, in1, p7, both = lax.optimization_barrier(
        (got, leg, in0, in1, rest[4], project(pair, w_in))
    )
    own = exchange(both)
    own, p7 = lax.optimization_barrier((own, p7))
    got[7], crossed = lax.optimization_barrier((direct(7, p7), cross(own, row_count, high)))
    returned = exchange(crossed)
    got[0] = jnp.where(is_far, leg[:rows], in0)
    got[1] = jnp.where(is_far, leg[rows:], in1)
    turned = place([got[s] for s in range(low)])
    return finish(returned, turned, gate_of(turned, w_gate), w_out)


def solution(mesh):
    placed = (P("row", "col", None), P(), P(), P())
    return jax.shard_map(
        on_device, mesh=mesh, in_specs=placed, out_specs=P("row", "col", None), check_vma=False
    )
```

```python
import jax
import jax.numpy as jnp
from jax import lax
from jax.experimental import pallas as pl
from jax.experimental.pallas import tpu as pltpu
from jax.sharding import PartitionSpec as P

ALL = ("row", "col")
GB = 16
PITCH = 24


def sigmoid(x):
    return 0.5 * jnp.tanh(0.5 * x) + 0.5


def params(mib):
    return pltpu.CompilerParams(vmem_limit_bytes=mib * 1024 * 1024)


def project_kernel(x_ref, wt_ref, o_ref, sa, sb):
    groups = x_ref.shape[0]
    hidden = o_ref.shape[0]

    for g in range(0, groups, 2):
        parts = []
        for q in range(2):
            v = x_ref[g + q].T.astype(jnp.float32)
            mean = jnp.mean(v, axis=0, keepdims=True)
            v = v - mean
            var = jnp.mean(v * v, axis=0, keepdims=True)
            parts.append((v * lax.rsqrt(var + 1e-5)).astype(jnp.bfloat16))
        n = jnp.concatenate(parts, axis=1)
        for dst, k in ((sa, 0), (sb, 2)):
            gate = jnp.dot(wt_ref[pl.ds(k * hidden, hidden), :], n, preferred_element_type=jnp.float32)
            value = jnp.dot(
                wt_ref[pl.ds((k + 1) * hidden, hidden), :], n, preferred_element_type=jnp.float32
            )
            res = sigmoid(gate) * value
            for q in range(2):
                dst[pl.ds(g + q, hidden, stride=groups), :] = res[:, q * 128 : (q + 1) * 128]
    for p, src in ((0, sa), (1, sb)):
        o_ref[:, p] = src[...].astype(jnp.bfloat16).reshape(hidden, groups, 128)


def project(pair, w_in):
    rows, cols, width = pair.shape
    hidden = w_in.shape[1] // 4
    kg = cols // 128
    return pl.pallas_call(
        project_kernel,
        grid=(kg, rows // GB),
        in_specs=[
            pl.BlockSpec((GB, 128, width), lambda k, i: (i, k, 0)),
            pl.BlockSpec((4 * hidden, width), lambda k, i: (0, 0)),
        ],
        out_specs=pl.BlockSpec((hidden, None, 2, GB, 128), lambda k, i: (0, k, 0, i, 0)),
        out_shape=jax.ShapeDtypeStruct((hidden, kg, 2, rows, 128), jnp.bfloat16),
        scratch_shapes=[pltpu.VMEM((hidden * GB, 128), jnp.float32)] * 2,
        compiler_params=params(16),
        cost_estimate=pl.CostEstimate(
            flops=2 * rows * cols * width * hidden * 4,
            bytes_accessed=6 * rows * cols * width,
            transcendentals=2 * rows * cols * hidden,
        ),
        name="project",
    )(pair, w_in.T)


def plane_rows(ref):
    count, kgs, rows, lanes = ref.shape
    return jnp.concatenate([ref[:, q].reshape(count * rows, lanes) for q in range(kgs)], axis=1)


def cross_kernel(b_ref, a_ref, o_ref):
    row_count, parts, kg, group, _ = o_ref.shape
    res = lax.dot_general(
        plane_rows(b_ref),
        plane_rows(a_ref),
        (((1,), (1,)), ((), ())),
        preferred_element_type=jnp.float32,
    ).astype(jnp.bfloat16)
    for t in range(kg):
        o_ref[:, :, t] = res[:, t * 128 : (t + 1) * 128].reshape(row_count, parts, group, 128)


def cross(own, row_count, col_count):
    _, kg, _, rows, _ = own.shape
    group = GB
    parts = rows // group
    kgs = col_count * kg
    own = own.reshape(row_count, kgs, 2, rows, 128)
    low = row_count // col_count
    tokens = row_count * rows
    return pl.pallas_call(
        cross_kernel,
        grid=(col_count,),
        in_specs=[
            pl.BlockSpec((row_count, kgs, None, rows, 128), lambda c: (0, 0, 1, 0, 0)),
            pl.BlockSpec((low, kgs, None, rows, 128), lambda c: (c, 0, 0, 0, 0)),
        ],
        out_specs=pl.BlockSpec(
            (row_count, None, parts, kg, group, 128), lambda c: (0, c, 0, 0, 0, 0)
        ),
        out_shape=jax.ShapeDtypeStruct(
            (row_count, col_count, parts, kg, group, 128), jnp.bfloat16
        ),
        compiler_params=params(56),
        cost_estimate=pl.CostEstimate(
            flops=2 * tokens**3, bytes_accessed=6 * tokens * tokens, transcendentals=0
        ),
        name="cross",
    )(own, own).reshape(row_count * col_count, parts, kg, group, 128)


def gate_kernel(z_ref, w_ref, g_ref):
    jb, cols, width = z_ref.shape
    z = z_ref[...].reshape(jb * cols, width).astype(jnp.float32)
    mean = jnp.mean(z, axis=-1, keepdims=True)
    z = z - mean
    var = jnp.mean(z * z, axis=-1, keepdims=True)
    n = (z * lax.rsqrt(var + 1e-5)).astype(jnp.bfloat16)
    gate = sigmoid(jnp.dot(n, w_ref[...], preferred_element_type=jnp.float32))
    g_ref[...] = gate.astype(g_ref.dtype).reshape(g_ref.shape)


def gate_of(z, w_gate):
    rows, cols, width = z.shape
    jb = 4
    return pl.pallas_call(
        gate_kernel,
        grid=(rows // jb,),
        in_specs=[
            pl.BlockSpec((jb, cols, width), lambda j: (j, 0, 0)),
            pl.BlockSpec((width, width), lambda j: (0, 0)),
        ],
        out_specs=pl.BlockSpec((jb, cols, width), lambda j: (j, 0, 0)),
        out_shape=jax.ShapeDtypeStruct((rows, cols, width), jnp.bfloat16),
        compiler_params=params(12),
        cost_estimate=pl.CostEstimate(
            flops=2 * rows * cols * width * width,
            bytes_accessed=6 * rows * cols * width,
            transcendentals=rows * cols * width,
        ),
        name="gate",
    )(z, w_gate)


def finish_kernel(r_ref, z_ref, g_ref, w_ref, o_ref, scr):
    hidden, groups, jb, _ = r_ref.shape
    width = w_ref.shape[1]
    batch = 4
    for t in range(groups):
        v = r_ref[:, t].astype(jnp.float32)
        v = v - jnp.mean(v, axis=0, keepdims=True)
        var = jnp.mean(v * v, axis=0, keepdims=True)
        scr.reshape(hidden, PITCH, 128)[:, :jb, :] = v * lax.rsqrt(var + 1e-5)
        for first in range(0, jb, batch):
            parts = [
                scr[pl.ds(j, hidden, stride=PITCH), :].astype(jnp.bfloat16)
                for j in range(first, first + batch)
            ]
            update = lax.dot_general(
                jnp.concatenate(parts, axis=1),
                w_ref[...],
                (((0,), (0,)), ((), ())),
                preferred_element_type=jnp.float32,
            ).reshape(batch, 128, width)
            at = (pl.ds(first, batch), pl.ds(t * 128, 128))
            res = z_ref[at].astype(jnp.float32) + g_ref[at].astype(jnp.float32) * update
            o_ref[at] = res.astype(jnp.bfloat16)


def finish(returned, z, gate, w_out):
    hidden, parts, groups, jb, _ = returned.shape
    rows, cols, width = z.shape
    tok = pl.BlockSpec((jb, cols, width), lambda j: (j, 0, 0))
    return pl.pallas_call(
        finish_kernel,
        grid=(parts,),
        in_specs=[
            pl.BlockSpec((hidden, None, groups, jb, 128), lambda j: (0, j, 0, 0, 0)),
            tok,
            tok,
            pl.BlockSpec((hidden, width), lambda j: (0, 0)),
        ],
        out_specs=tok,
        out_shape=jax.ShapeDtypeStruct((rows, cols, width), jnp.bfloat16),
        scratch_shapes=[pltpu.VMEM((hidden * PITCH, 128), jnp.float32)],
        compiler_params=params(56),
        cost_estimate=pl.CostEstimate(
            flops=2 * rows * cols * width * hidden,
            bytes_accessed=8 * rows * cols * width,
            transcendentals=0,
        ),
        name="finish",
    )(returned, z, gate, w_out)


def cut(pair, low):
    rows, cols, width = pair.shape
    me = lax.rem(lax.axis_index("row"), low)
    pieces = pair.reshape(rows, low, rows, width)
    return [
        lax.dynamic_index_in_dim(pieces, lax.bitwise_xor(me, s), 1, keepdims=False)
        for s in range(low)
    ]


def send(piece, low, high, target, chosen=lambda h, q, c: True):
    perm = []
    for h in range(high):
        for q in range(low):
            for c in range(high):
                if chosen(h, q, c):
                    th, tq, tc = target(h, q, c)
                    perm.append(((h * low + q) * high + c, (th * low + tq) * high + tc))
    return lax.ppermute(piece, ALL, perm)


def near(h, q, c):
    return h // 2 == c // 2


def far(h, q, c):
    return not near(h, q, c)


def final(s):
    return lambda h, q, c: (c, q ^ s, h)


def halfway(s):
    return lambda h, q, c: (c, q ^ s, c // 2 * 2 + h % 2)


def onward(h, q, c):
    return h, q, c ^ 2


def place(moved):
    low = len(moved)
    rows, _, width = moved[0].shape
    me = lax.rem(lax.axis_index("row"), low)
    got = jnp.zeros((low, rows, rows, width), moved[0].dtype)
    for s, piece in enumerate(moved):
        got = lax.dynamic_update_index_in_dim(got, piece, lax.bitwise_xor(me, s), 0)
    return jnp.transpose(got, (2, 0, 1, 3)).reshape(rows, low * rows, width)


def exchange(x):
    return lax.all_to_all(x, ALL, split_axis=0, concat_axis=0, tiled=True)


def on_device(pair, w_in, w_gate, w_out):
    row_count = lax.axis_size("row")
    high = lax.axis_size("col")
    low = row_count // high
    rows = pair.shape[0]
    is_far = lax.axis_index("row") // low // 2 != lax.axis_index("col") // 2
    p = cut(pair, low)

    def direct(s, piece):
        return send(piece, low, high, final(s))

    def inner(s, piece):
        return send(piece, low, high, final(s), near)

    def first_leg(s, piece):
        return send(piece, low, high, halfway(s), far)

    def second_leg(piece):
        return send(piece, low, high, onward, near)

    half0, half1 = first_leg(0, p[0]), first_leg(1, p[1])
    got = {s: direct(s, p[s]) for s in (2, 3)}
    in0 = inner(0, p[0])
    half0, half1, rest = lax.optimization_barrier((half0, half1, [p[s] for s in (1, 4, 5, 6, 7)]))
    leg = second_leg(jnp.concatenate([half0, half1], axis=0))
    for s in (4, 5, 6):
        got[s] = direct(s, rest[s - 3])
    in1 = inner(1, rest[0])
    got, leg, in0, in1, p7, both = lax.optimization_barrier(
        (got, leg, in0, in1, rest[4], project(pair, w_in))
    )
    own = exchange(both)
    own, p7 = lax.optimization_barrier((own, p7))
    got[7], crossed = lax.optimization_barrier((direct(7, p7), cross(own, row_count, high)))
    returned = exchange(crossed)
    got[0] = jnp.where(is_far, leg[:rows], in0)
    got[1] = jnp.where(is_far, leg[rows:], in1)
    turned = place([got[s] for s in range(low)])
    return finish(returned, turned, gate_of(turned, w_gate), w_out)


def solution(mesh):
    placed = (P("row", "col", None), P(), P(), P())
    return jax.shard_map(
        on_device, mesh=mesh, in_specs=placed, out_specs=P("row", "col", None), check_vma=False
    )
```
